512 devices in a mesh: bas: 128 (over y, z, core), orb: 4 (over x).
Axes of the slice: x: 4, y: 8, z: 8, core: 2. Of those that a mesh axis runs over, the one named last changes fastest.
Arguments:
- orbitals: bfloat16 [16384, 1024], P('bas', 'orb'), may hold values from -0.046875 to 0.046875
- dipole_orbitals: bfloat16 [3, 16384, 1024], P(None, 'bas', 'orb'), may hold values from -6 to 6
- generator: bfloat16 [1024, 1024], P(None, 'orb'), may hold values from -0.42 to 0.42, as said below
- integrals: bfloat16 [128, 1024, 4096], P('bas', None, 'orb'), may hold values from -6 to 6
Outputs:
- new_orbitals: bfloat16 [16384, 1024], P('bas', 'orb')
- regrouped: bfloat16 [128, 1024, 4096], P(None, 'bas', 'orb')
The draws below stay inside these ranges and needn't reach their ends.
Inputs may be any that keep to these rules, and one draw needn't show every extreme that they name: generator is antisymmetric: generator[i, j] = -generator[j, i].
All inputs are finite; a program needn't handle non-finite values.
Results may differ from the reference program's by a relative error of at most 0.0049.
Values may be sent and summed in bfloat16 or wider, within the bound.
No kernel may reach another device: no remote copies, remote signals or barrier semaphores. Data moves between devices by JAX's collectives and lax.ppermute only.
A program may use at most 128 MiB of HBM per device.

```python
import jax
import jax.numpy as jnp
from jax import lax

NOCC = 1024
NVIRT = 4096
ORDER = 6
NBAS = 16384
NAUX = 128


def draw_generator(key, part):
    key = jax.random.fold_in(key, 7)
    base = jnp.clip(jax.random.normal(key, (NOCC, NOCC), jnp.float32), -6.0, 6.0)
    return ((base - base.T) * 0.035).astype(jnp.bfloat16)


def shard_levels(stream_key, shape, pieces, least, high):
    level = 1.0
    for position, blocks in pieces:
        draws = jax.random.uniform(jax.random.fold_in(jax.random.fold_in(stream_key, 6), position), (blocks,), jnp.float32, least / len(pieces), high / len(pieces))
        level = level * jnp.repeat(jnp.exp(draws), shape[position] // blocks).reshape((-1,) + (1,) * (len(shape) - 1 - position))
    return level


def normal_values(rng, extent, spread, reach, cuts=(), kind=jnp.bfloat16):
    entries = jax.random.normal(rng, extent, jnp.float32) * spread
    if len(cuts) > 0:
        entries = shard_levels(rng, extent, cuts, -0.22, 0.18) * entries
    return jnp.clip(entries, min=-reach, max=reach).astype(kind)


def setup_inputs(seed: int = 0) -> dict:
    streams_of = jax.random.split(jax.random.key(seed), 5)
    orbitals = normal_values(streams_of[0], (NBAS, NOCC), NBAS ** -0.5, 0.046875, ((0, 128), (1, 4)))
    dipole_orbitals = normal_values(streams_of[1], (3, NBAS, NOCC), 1.0, 6.0, ((1, 128), (2, 4)))
    generator = draw_generator(jax.random.fold_in(streams_of[4], 71), 0)
    integrals = normal_values(streams_of[3], (NAUX, NOCC, NVIRT), 1.0, 6.0, ((0, 128), (2, 4)))
    return {"orbitals": orbitals, "dipole_orbitals": dipole_orbitals, "generator": generator, "integrals": integrals}


def reference(orbitals, dipole_orbitals, generator, integrals):
    moments = jnp.stack([jnp.dot(orbitals.T, dipole_orbitals[k], preferred_element_type=jnp.float32) for k in range(3)])
    centers = jnp.stack([jnp.diagonal(moments[k]) for k in range(3)])
    gradient = 4.0 * lax.optimization_barrier(jnp.sum(moments * (centers[:, :, None] - centers[:, None, :]), axis=0))
    rotation_gen = gradient / (16.0 * jnp.sqrt(jnp.float32(NOCC))) + generator.astype(jnp.float32)
    term = jnp.eye(NOCC, dtype=jnp.float32)
    total = term
    for step in range(ORDER):
        term = jnp.dot(rotation_gen, term, precision=lax.Precision.HIGHEST) / (step + 1.0)
        total = total + term
    rotation = total.astype(jnp.bfloat16)
    new_orbitals = jnp.dot(orbitals, rotation, preferred_element_type=jnp.float32).astype(jnp.bfloat16)

    def rotate_one(block):
        return jnp.dot(rotation.T, block, preferred_element_type=jnp.float32).astype(jnp.bfloat16)
    regrouped = lax.map(rotate_one, integrals)
    return (new_orbitals, regrouped)
```

```python
import functools

import jax
import jax.numpy as jnp
from jax import lax
from jax.experimental import pallas as pl
from jax.experimental.pallas import tpu as pltpu
from jax.sharding import Mesh, PartitionSpec as P

F32, BF16, F16 = jnp.float32, jnp.bfloat16, jnp.float16
PLANE = ("y", "z")
BAS = ("y", "z", "core")
WIRE_SCALE = 0.0625


def high_low(value):
    high = value.astype(BF16)
    return high, (value - high.astype(F32)).astype(BF16)


def gradient_kernel(scale, c_own, c_other, d_own, d_other, cen_i, cen_j, out):
    contract = (((0,), (0,)), ((), ()))
    for half in range(c_own.shape[0]):
        cols = slice(256 * half, 256 * half + 256)
        total = None
        for k in range(3):
            moment = lax.dot_general(d_own[k], c_own[half], contract, preferred_element_type=F32)
            moment += lax.dot_general(d_other[k], c_other[half], contract, preferred_element_type=F32)
            term = moment * (cen_i[k : k + 1, cols] - cen_j[:, k : k + 1])
            total = term if total is None else total + term
        total = total * scale
        for r in range(16):
            for g in range(2):
                out[4 * r + 2 * half + g] = total[16 * r : 16 * r + 16, 128 * g : 128 * g + 128]


def product(left_h, left_l, right_h, right_l):
    dot = functools.partial(jnp.dot, preferred_element_type=F32)
    return dot(left_h, right_h) + (dot(left_h, right_l) + dot(left_l, right_h))


def series_kernel(
    place, own_h, own_l, other_h, other_l, integrals, orb, rotated, new_orb,
    xh, xl, x2, x2h, x2l, x3h, x3l, qh, ql, rot,
):
    n, tile = 1024, 256
    core, orb_index = place[0], place[1]
    for src_h, src_l, half in ((own_h, own_l, core), (other_h, other_l, 1 - core)):
        for g in range(4):
            cols = pl.ds(pl.multiple_of(half * 512 + 128 * g, 128), 128)
            for xi in range(4):
                for r in range(16):
                    rows = slice(256 * xi + 16 * r, 256 * xi + 16 * r + 16)
                    xh[rows, cols] = src_h[xi, 4 * r + g]
                    xl[rows, cols] = src_l[xi, 4 * r + g]

    def identity(first):
        row = lax.broadcasted_iota(jnp.int32, (n, tile), 0)
        col = lax.broadcasted_iota(jnp.int32, (n, tile), 1) + first
        return (row == col).astype(F32)

    @pl.loop(0, n // tile)
    def _(step):
        cols = pl.ds(pl.multiple_of(step * tile, tile), tile)
        block = product(xh[...], xl[...], xh[:, cols], xl[:, cols])
        x2[:, cols] = block
        x2h[:, cols], x2l[:, cols] = high_low(block)

    @pl.loop(0, n // tile)
    def _(step):
        cols = pl.ds(pl.multiple_of(step * tile, tile), tile)
        block = product(xh[...], xl[...], x2h[:, cols], x2l[:, cols])
        x3h[:, cols], x3l[:, cols] = high_low(block)
        x1 = xh[:, cols].astype(F32) + xl[:, cols].astype(F32)
        rest = identity(step * tile) * (1 / 6) + x1 * (1 / 24) + x2[:, cols] * (1 / 120) + block * (1 / 720)
        qh[:, cols], ql[:, cols] = high_low(rest)

    @pl.loop(0, n // tile)
    def _(step):
        cols = pl.ds(pl.multiple_of(step * tile, tile), tile)
        block = product(x3h[...], x3l[...], qh[:, cols], ql[:, cols])
        x1 = xh[:, cols].astype(F32) + xl[:, cols].astype(F32)
        rot[:, cols] = (block + 0.5 * x2[:, cols] + x1 + identity(step * tile)).astype(BF16)

    @pl.loop(0, n // tile)
    def _(step):
        cols = pl.ds(pl.multiple_of(step * tile, tile), tile)
        rotated[:, cols] = jnp.dot(rot[...], integrals[:, cols], preferred_element_type=F32).astype(BF16)

    own = rot[pl.ds(pl.multiple_of(orb_index * 256, 256), 256), :]
    total = None
    for xi in range(4):
        part = lax.dot_general(
            orb[xi], own[:, 256 * xi : 256 * xi + 256], (((1,), (1,)), ((), ())), preferred_element_type=F32
        )
        total = part if total is None else total + part
    new_orb[...] = total.astype(BF16)


def on_device(orbitals, dipole_orbitals, generator, integrals):
    nbas, block = orbitals.shape
    nocc = generator.shape[0]
    scale = 4.0 / (16.0 * nocc**0.5)
    core, orb_index = lax.axis_index("core"), lax.axis_index("x")
    place = lax.axis_index("y") * 8 + lax.axis_index("z")
    swap = [(0, 1), (1, 0)]

    def spread(value, axes, count):
        copies = jnp.broadcast_to(value[None], (count,) + value.shape)
        return lax.all_to_all(copies, axes, 0, 0, tiled=True)

    d_other = lax.ppermute(dipole_orbitals, "core", swap)

    partial = jnp.sum(orbitals.astype(F32)[None] * dipole_orbitals.astype(F32), axis=1)
    summed = jnp.sum(spread(partial, PLANE, 64), axis=0)
    first = lax.reduce_precision(summed, 8, 7)
    second = lax.reduce_precision(summed - first, 8, 7)
    third = summed - first - second
    parts = jnp.concatenate([first, second, third, jnp.zeros((7, block), F32)], axis=0).astype(BF16)
    met = spread(jnp.concatenate([orbitals, parts], axis=0), ("core", "x"), 8).reshape(2, 4, nbas + 16, block)
    c_own = lax.dynamic_index_in_dim(met, core, 0, keepdims=False)
    c_other = lax.dynamic_index_in_dim(met, 1 - core, 0, keepdims=False)
    cen = met[:, :, nbas : nbas + 9].astype(F32).reshape(2, 4, 3, 3, block)
    cen = cen[:, :, 0] + cen[:, :, 1] + cen[:, :, 2]
    cen = (cen[0] + cen[1]).transpose(1, 0, 2).reshape(3, nocc)
    cen_i = lax.dynamic_slice_in_dim(cen, core * 512, 512, 1)
    cen_j = lax.dynamic_slice_in_dim(cen, orb_index * block, block, 1).T

    pieces = pl.pallas_call(
        functools.partial(gradient_kernel, scale),
        out_shape=jax.ShapeDtypeStruct((64, 16, 128), F32),
        name="gradient",
    )(
        lax.dynamic_slice_in_dim(c_own[:, :nbas], 2 * core, 2, 0),
        lax.dynamic_slice_in_dim(c_other[:, :nbas], 2 * core, 2, 0),
        dipole_orbitals, d_other, cen_i, cen_j,
    )
    given = lax.dynamic_slice(
        generator, (core * 512 + (place % 4) * 128, (place // 4) * 16), (128, 16)
    ).astype(F32).T
    piece = jnp.sum(lax.all_to_all(pieces, PLANE, 0, 0, tiled=True), axis=0) + given
    wire = (piece * WIRE_SCALE).astype(F16)
    half = spread(spread(wire, PLANE, 64), "x", 4)
    other = lax.ppermute(half, "core", swap)

    def pair(value):
        value = value.astype(F32) * (1 / WIRE_SCALE)
        high = lax.reduce_precision(value, 8, 7)
        return high.astype(BF16), (value - high).astype(BF16)

    n = nocc
    vmem = pl.BlockSpec(memory_space=pltpu.VMEM)
    rotated, new_orbitals = pl.pallas_call(
        series_kernel,
        out_shape=(jax.ShapeDtypeStruct((n, n), BF16), jax.ShapeDtypeStruct((nbas, block), BF16)),
        in_specs=[pl.BlockSpec(memory_space=pltpu.SMEM)] + [vmem] * 6,
        out_specs=(vmem, vmem),
        scratch_shapes=[
            pltpu.VMEM((n, n), BF16), pltpu.VMEM((n, n), BF16), pltpu.VMEM((n, n), F32),
            pltpu.VMEM((n, n), BF16), pltpu.VMEM((n, n), BF16), pltpu.VMEM((n, n), BF16),
            pltpu.VMEM((n, n), BF16), pltpu.VMEM((n, n), BF16), pltpu.VMEM((n, n), BF16),
            pltpu.VMEM((n, n), BF16),
        ],
        compiler_params=pltpu.CompilerParams(vmem_limit_bytes=56 << 20),
        name="series",
    )(jnp.stack([core, orb_index]).astype(jnp.int32), *pair(half), *pair(other), integrals[0], c_own[:, :nbas])
    regrouped = lax.all_to_all(rotated.reshape(128, 8, n), BAS, 0, 0, tiled=True)
    return new_orbitals, regrouped


def solution(mesh):
    split = Mesh(mesh.devices.reshape(8, 8, 2, 4), ("y", "z", "core", "x"))
    return jax.shard_map(
        on_device,
        mesh=split,
        in_specs=(P(BAS, "x"), P(None, BAS, "x"), P(None, "x"), P(BAS, None, "x")),
        out_specs=(P(BAS, "x"), P(None, BAS, "x")),
        check_vma=False,
    )
```

```python
import functools

import jax
import jax.numpy as jnp
from jax import lax
from jax.experimental import pallas as pl
from jax.experimental.pallas import tpu as pltpu
from jax.sharding import Mesh, PartitionSpec as P

F32, BF16, F16 = jnp.float32, jnp.bfloat16, jnp.float16
PLANE = ("y", "z")
BAS = ("y", "z", "core")
WIRE_SCALE = 0.0625
def grant(mib):
    return pltpu.CompilerParams(vmem_limit_bytes=mib << 20)


VMEM = pl.BlockSpec(memory_space=pltpu.VMEM)
SMEM = pl.BlockSpec(memory_space=pltpu.SMEM)


def high_low(value):
    high = value.astype(BF16)
    return high, (value - high.astype(F32)).astype(BF16)


def diagonal_kernel(orb, dip, out):
    for k in range(3):
        part = jnp.sum(orb[...].astype(F32) * dip[k].astype(F32), axis=0, keepdims=True)
        for half in range(2):
            line = jnp.broadcast_to(part[:, 128 * half : 128 * half + 128], (out.shape[0], 128))
            out[:, 2 * k + half] = line
    out[:, 6:8] = jnp.zeros((out.shape[0], 2, 128), F32)


def pack_kernel(parts, orb, out):
    total = jnp.sum(parts[...], axis=0)
    first = total.astype(BF16)
    rest = total - first.astype(F32)
    second = rest.astype(BF16)
    third = (rest - second.astype(F32)).astype(BF16)
    tail = jnp.concatenate([first, second, third, jnp.zeros((8, 128), BF16)], axis=0)
    for d in range(out.shape[0]):
        out[d, 0, :128] = orb[:, :128]
        out[d, 1, :128] = orb[:, 128:]
        out[d, 0, 128:] = tail
        out[d, 1, 128:] = jnp.zeros((32, 128), BF16)


def gradient_kernel(scale, place, met, d_own, d_other, out):
    core, orb = place[0], place[1]
    contract = (((0,), (0,)), ((), ()))

    def centers(block):
        total = jnp.zeros((8, 128), F32)
        for source in range(2):
            tail = met[4 * source + block, 0, 128:].astype(F32)
            total = total + (tail[0:8] + tail[8:16] + tail[16:24])
        return total

    mine = centers(orb)
    turned = mine.T
    cen_j = [jnp.concatenate([turned[:, 2 * k : 2 * k + 1], turned[:, 2 * k + 1 : 2 * k + 2]], axis=0) for k in range(3)]
    for half in range(2):
        block = 2 * core + half
        cen_i = centers(block)
        for g in range(2):
            total = None
            for k in range(3):
                moment = lax.dot_general(d_own[k], met[4 * core + block, g, :128], contract, preferred_element_type=F32)
                moment += lax.dot_general(
                    d_other[k], met[4 * (1 - core) + block, g, :128], contract, preferred_element_type=F32
                )
                term = moment * (cen_i[2 * k + g : 2 * k + g + 1] - cen_j[k])
                total = term if total is None else total + term
            total = total * scale
            for r in range(16):
                out[4 * r + 2 * half + g] = total[16 * r : 16 * r + 16]


def product(left_h, left_l, right_h, right_l):
    dot = functools.partial(jnp.dot, preferred_element_type=F32)
    return dot(left_h, right_h) + (dot(left_h, right_l) + dot(left_l, right_h))


def series_kernel(place, own_h, own_l, other_h, other_l, rot, xh, xl, x2h, x2l, qh, ql):
    n, tile = 1024, 256
    core = place[0]
    for src_h, src_l, half in ((own_h, own_l, core), (other_h, other_l, 1 - core)):
        for g in range(4):
            cols = pl.ds(pl.multiple_of(half * 512 + 128 * g, 128), 128)
            for xi in range(4):
                for r in range(16):
                    rows = slice(256 * xi + 16 * r, 256 * xi + 16 * r + 16)
                    xh[rows, cols] = src_h[xi, 4 * r + g]
                    xl[rows, cols] = src_l[xi, 4 * r + g]

    def one(first):
        row = lax.broadcasted_iota(jnp.int32, (n, tile), 0)
        col = lax.broadcasted_iota(jnp.int32, (n, tile), 1) + first
        return (row == col).astype(F32)

    def linear(cols):
        return xh[:, cols].astype(F32) + xl[:, cols].astype(F32)

    @pl.loop(0, n // tile)
    def _(step):
        cols = pl.ds(pl.multiple_of(step * tile, tile), tile)
        square = product(xh[...], xl[...], xh[:, cols], xl[:, cols])
        x2h[:, cols], x2l[:, cols] = high_low(square)
        qh[:, cols], ql[:, cols] = high_low(
            one(step * tile) * (1 / 24) + linear(cols) * (1 / 120) + square * (1 / 720)
        )

    @pl.loop(0, 2)
    def _(step):
        first = core * 512 + step * tile
        cols = pl.ds(pl.multiple_of(first, tile), tile)
        inner = product(x2h[...], x2l[...], qh[:, cols], ql[:, cols])
        qh[:, cols], ql[:, cols] = high_low(one(first) * 0.5 + linear(cols) * (1 / 6) + inner)

    @pl.loop(0, 2)
    def _(step):
        first = core * 512 + step * tile
        cols = pl.ds(pl.multiple_of(first, tile), tile)
        outer = product(x2h[...], x2l[...], qh[:, cols], ql[:, cols])
        rot[:, pl.ds(pl.multiple_of(step * tile, tile), tile)] = (one(first) + linear(cols) + outer).astype(BF16)


def rotate_kernel(place, rot_own, rot_other, integrals, out):
    core, tile = place[0], 256
    near = pl.ds(pl.multiple_of(core * 512, 512), 512)
    far = pl.ds(pl.multiple_of(512 - core * 512, 512), 512)

    @pl.loop(0, 1024 // tile)
    def _(step):
        cols = pl.ds(pl.multiple_of(step * tile, tile), tile)
        total = jnp.dot(rot_own[...], integrals[near, cols], preferred_element_type=F32)
        total += jnp.dot(rot_other[...], integrals[far, cols], preferred_element_type=F32)
        out[:, cols] = total.astype(BF16)


def orbitals_kernel(place, rot_own, rot_other, met, out):
    core, orb = place[0], place[1]
    rows = pl.ds(pl.multiple_of(orb * 256, 256), 256)
    total = None
    for rot, half in ((rot_own, core), (rot_other, 1 - core)):
        mine = rot[rows, :]
        for h in range(2):
            for g in range(2):
                first = 256 * h + 128 * g
                part = lax.dot_general(
                    met[4 * core + 2 * half + h, g, :128], mine[:, first : first + 128],
                    (((1,), (1,)), ((), ())), preferred_element_type=F32,
                )
                total = part if total is None else total + part
    out[...] = total.astype(BF16)


def on_device(orbitals, dipole_orbitals, generator, integrals):
    nbas, block = orbitals.shape
    nocc = generator.shape[0]
    scale = 4.0 / (16.0 * nocc**0.5)
    core, orb_index = lax.axis_index("core"), lax.axis_index("x")
    spot = lax.axis_index("y") * 8 + lax.axis_index("z")
    place = jnp.stack([core, orb_index]).astype(jnp.int32)
    swap = [(0, 1), (1, 0)]

    def spread(value, axes, count):
        copies = jnp.broadcast_to(value[None], (count,) + value.shape)
        return lax.all_to_all(copies, axes, 0, 0, tiled=True)

    partial = pl.pallas_call(
        diagonal_kernel, out_shape=jax.ShapeDtypeStruct((64, 8, 128), F32), name="diagonal"
    )(orbitals, dipole_orbitals)
    partial, d_here, given = lax.optimization_barrier((partial, dipole_orbitals, generator))
    centers = lax.all_to_all(partial, PLANE, 0, 0, tiled=True)
    d_other = lax.ppermute(d_here, "core", swap)
    centers, d_other = lax.optimization_barrier((centers, d_other))
    given = lax.dynamic_slice(given, (core * 512 + (spot % 4) * 128, (spot // 4) * 16), (128, 16)).astype(F32).T
    packed = pl.pallas_call(
        pack_kernel, out_shape=jax.ShapeDtypeStruct((8, 2, nbas + 32, 128), BF16), compiler_params=grant(6), name="pack"
    )(centers, orbitals)
    packed, d_here, given = lax.optimization_barrier((packed, d_here, given))
    met = lax.all_to_all(packed, ("core", "x"), 0, 0, tiled=True)
    pieces = pl.pallas_call(
        functools.partial(gradient_kernel, scale),
        out_shape=jax.ShapeDtypeStruct((64, 16, 128), F32),
        in_specs=[SMEM] + [VMEM] * 3,
        compiler_params=grant(8),
        name="gradient",
    )(place, met, d_here, d_other)
    piece = jnp.sum(lax.all_to_all(pieces, PLANE, 0, 0, tiled=True), axis=0) + given
    wire = (piece * WIRE_SCALE).astype(F16)
    half = spread(spread(wire, PLANE, 64), "x", 4)
    other = lax.ppermute(half, "core", swap)

    def pair(value):
        value = value.astype(F32) * (1 / WIRE_SCALE)
        high = lax.reduce_precision(value, 8, 7)
        return high.astype(BF16), (value - high).astype(BF16)

    n = nocc
    rot_own = pl.pallas_call(
        series_kernel,
        out_shape=jax.ShapeDtypeStruct((n, n // 2), BF16),
        in_specs=[SMEM] + [VMEM] * 4,
        scratch_shapes=[pltpu.VMEM((n, n), BF16)] * 6,
        compiler_params=grant(24),
        name="series",
    )(place, *pair(half), *pair(other))
    rot_other = lax.ppermute(rot_own, "core", swap)
    rotated = pl.pallas_call(
        rotate_kernel,
        out_shape=jax.ShapeDtypeStruct((n, n), BF16),
        in_specs=[SMEM] + [VMEM] * 3,
        compiler_params=grant(16),
        name="rotate",
    )(place, rot_own, rot_other, integrals[0])
    regrouped = lax.all_to_all(rotated.reshape(128, 8, n), BAS, 0, 0, tiled=True)
    new_orbitals = pl.pallas_call(
        orbitals_kernel,
        out_shape=jax.ShapeDtypeStruct((nbas, block), BF16),
        in_specs=[SMEM] + [VMEM] * 3,
        compiler_params=grant(8),
        name="new_orbitals",
    )(place, rot_own, rot_other, met)
    return new_orbitals, regrouped


def solution(mesh):
    split = Mesh(mesh.devices.reshape(8, 8, 2, 4), ("y", "z", "core", "x"))
    return jax.shard_map(
        on_device,
        mesh=split,
        in_specs=(P(BAS, "x"), P(None, BAS, "x"), P(None, "x"), P(BAS, None, "x")),
        out_specs=(P(BAS, "x"), P(None, BAS, "x")),
        check_vma=False,
    )
```

```python
import functools

import jax
import jax.numpy as jnp
from jax import lax
from jax.experimental import pallas as pl
from jax.experimental.pallas import tpu as pltpu
from jax.sharding import Mesh, PartitionSpec as P

F32, BF16, F16 = jnp.float32, jnp.bfloat16, jnp.float16
PLANE = ("y", "z")
BAS = ("y", "z", "core")
WIRE_SCALE = 0.0625
def grant(mib):
    return pltpu.CompilerParams(vmem_limit_bytes=mib << 20)


VMEM = pl.BlockSpec(memory_space=pltpu.VMEM)
SMEM = pl.BlockSpec(memory_space=pltpu.SMEM)


def high_low(value):
    high = value.astype(BF16)
    return high, (value - high.astype(F32)).astype(BF16)


def diagonal_kernel(orb, dip, out):
    for k in range(3):
        part = jnp.sum(orb[...].astype(F32) * dip[k].astype(F32), axis=0, keepdims=True)
        for half in range(2):
            line = jnp.broadcast_to(part[:, 128 * half : 128 * half + 128], (out.shape[0], 128))
            out[:, 2 * k + half] = line
    out[:, 6:8] = jnp.zeros((out.shape[0], 2, 128), F32)


def pack_kernel(parts, orb, out):
    total = jnp.sum(parts[...], axis=0)
    first = total.astype(BF16)
    rest = total - first.astype(F32)
    second = rest.astype(BF16)
    third = (rest - second.astype(F32)).astype(BF16)
    tail = jnp.concatenate([first, second, third, jnp.zeros((8, 128), BF16)], axis=0)
    for d in range(out.shape[0]):
        out[d, 0, :128] = orb[:, :128]
        out[d, 1, :128] = orb[:, 128:]
        out[d, 0, 128:] = tail
        out[d, 1, 128:] = jnp.zeros((32, 128), BF16)


def gradient_kernel(scale, place, met, d_own, d_other, out):
    core, orb = place[0], place[1]
    contract = (((0,), (0,)), ((), ()))

    def centers(block):
        total = jnp.zeros((8, 128), F32)
        for source in range(2):
            tail = met[4 * source + block, 0, 128:].astype(F32)
            total = total + (tail[0:8] + tail[8:16] + tail[16:24])
        return total

    mine = centers(orb)
    turned = mine.T
    cen_j = [jnp.concatenate([turned[:, 2 * k : 2 * k + 1], turned[:, 2 * k + 1 : 2 * k + 2]], axis=0) for k in range(3)]
    for half in range(2):
        block = 2 * core + half
        cen_i = centers(block)
        for g in range(2):
            total = None
            for k in range(3):
                moment = lax.dot_general(d_own[k], met[4 * core + block, g, :128], contract, preferred_element_type=F32)
                moment += lax.dot_general(
                    d_other[k], met[4 * (1 - core) + block, g, :128], contract, preferred_element_type=F32
                )
                term = moment * (cen_i[2 * k + g : 2 * k + g + 1] - cen_j[k])
                total = term if total is None else total + term
            total = total * scale
            for r in range(16):
                out[4 * r + 2 * half + g] = total[16 * r : 16 * r + 16]


def product(left_h, left_l, right_h, right_l):
    dot = functools.partial(jnp.dot, preferred_element_type=F32)
    return dot(left_h, right_h) + (dot(left_h, right_l) + dot(left_l, right_h))


def series_kernel(place, own_h, own_l, other_h, other_l, rot, xh, xl, x2h, x2l, qh, ql):
    n, tile = 1024, 512
    core = place[0]
    for src_h, src_l, half in ((own_h, own_l, core), (other_h, other_l, 1 - core)):
        for g in range(4):
            cols = pl.ds(pl.multiple_of(half * 512 + 128 * g, 128), 128)
            for xi in range(4):
                for r in range(16):
                    rows = slice(256 * xi + 16 * r, 256 * xi + 16 * r + 16)
                    xh[rows, cols] = src_h[xi, 4 * r + g]
                    xl[rows, cols] = src_l[xi, 4 * r + g]

    def one(first):
        row = lax.broadcasted_iota(jnp.int32, (n, tile), 0)
        col = lax.broadcasted_iota(jnp.int32, (n, tile), 1) + first
        return (row == col).astype(F32)

    def linear(cols):
        return xh[:, cols].astype(F32) + xl[:, cols].astype(F32)

    @pl.loop(0, n // tile)
    def _(step):
        cols = pl.ds(pl.multiple_of(step * tile, tile), tile)
        square = product(xh[...], xl[...], xh[:, cols], xl[:, cols])
        x2h[:, cols], x2l[:, cols] = high_low(square)
        qh[:, cols], ql[:, cols] = high_low(
            one(step * tile) * (1 / 24) + linear(cols) * (1 / 120) + square * (1 / 720)
        )

    @pl.loop(0, 512 // tile)
    def _(step):
        first = core * 512 + step * tile
        cols = pl.ds(pl.multiple_of(first, tile), tile)
        inner = product(x2h[...], x2l[...], qh[:, cols], ql[:, cols])
        qh[:, cols], ql[:, cols] = high_low(one(first) * 0.5 + linear(cols) * (1 / 6) + inner)

    @pl.loop(0, 512 // tile)
    def _(step):
        first = core * 512 + step * tile
        cols = pl.ds(pl.multiple_of(first, tile), tile)
        outer = product(x2h[...], x2l[...], qh[:, cols], ql[:, cols])
        rot[:, pl.ds(pl.multiple_of(step * tile, tile), tile)] = (one(first) + linear(cols) + outer).astype(BF16)


def rotate_kernel(place, rot_own, rot_other, integrals, out):
    core, tile = place[0], 512
    near = pl.ds(pl.multiple_of(core * 512, 512), 512)
    far = pl.ds(pl.multiple_of(512 - core * 512, 512), 512)

    @pl.loop(0, 1024 // tile)
    def _(step):
        cols = pl.ds(pl.multiple_of(step * tile, tile), tile)
        total = jnp.dot(rot_own[...], integrals[near, cols], preferred_element_type=F32)
        total += jnp.dot(rot_other[...], integrals[far, cols], preferred_element_type=F32)
        out[:, cols] = total.astype(BF16)


def orbitals_kernel(place, rot_own, rot_other, met, out):
    core, orb = place[0], place[1]
    rows = pl.ds(pl.multiple_of(orb * 256, 256), 256)
    total = None
    for rot, half in ((rot_own, core), (rot_other, 1 - core)):
        mine = rot[rows, :]
        for h in range(2):
            for g in range(2):
                first = 256 * h + 128 * g
                part = lax.dot_general(
                    met[4 * core + 2 * half + h, g, :128], mine[:, first : first + 128],
                    (((1,), (1,)), ((), ())), preferred_element_type=F32,
                )
                total = part if total is None else total + part
    out[...] = total.astype(BF16)


def on_device(orbitals, dipole_orbitals, generator, integrals):
    nbas, block = orbitals.shape
    nocc = generator.shape[0]
    scale = 4.0 / (16.0 * nocc**0.5)
    core, orb_index = lax.axis_index("core"), lax.axis_index("x")
    spot = lax.axis_index("y") * 8 + lax.axis_index("z")
    place = jnp.stack([core, orb_index]).astype(jnp.int32)
    swap = [(0, 1), (1, 0)]

    def spread(value, axes, count):
        copies = jnp.broadcast_to(value[None], (count,) + value.shape)
        return lax.all_to_all(copies, axes, 0, 0, tiled=True)

    partial = pl.pallas_call(
        diagonal_kernel, out_shape=jax.ShapeDtypeStruct((64, 8, 128), F32), name="diagonal"
    )(orbitals, dipole_orbitals)
    partial, d_here, given = lax.optimization_barrier((partial, dipole_orbitals, generator))
    centers = lax.all_to_all(partial, PLANE, 0, 0, tiled=True)
    d_other = lax.ppermute(d_here, "core", swap)
    centers, d_other = lax.optimization_barrier((centers, d_other))
    given = lax.dynamic_slice(given, (core * 512 + (spot % 4) * 128, (spot // 4) * 16), (128, 16)).astype(F32).T
    packed = pl.pallas_call(
        pack_kernel, out_shape=jax.ShapeDtypeStruct((8, 2, nbas + 32, 128), BF16), compiler_params=grant(6), name="pack"
    )(centers, orbitals)
    packed, d_here, given = lax.optimization_barrier((packed, d_here, given))
    met = lax.all_to_all(packed, ("core", "x"), 0, 0, tiled=True)
    pieces = pl.pallas_call(
        functools.partial(gradient_kernel, scale),
        out_shape=jax.ShapeDtypeStruct((64, 16, 128), F32),
        in_specs=[SMEM] + [VMEM] * 3,
        compiler_params=grant(8),
        name="gradient",
    )(place, met, d_here, d_other)
    piece = jnp.sum(lax.all_to_all(pieces, PLANE, 0, 0, tiled=True), axis=0) + given
    wire = (piece * WIRE_SCALE).astype(F16)
    half = spread(spread(wire, PLANE, 64), "x", 4)
    other = lax.ppermute(half, "core", swap)

    def pair(value):
        value = value.astype(F32) * (1 / WIRE_SCALE)
        high = lax.reduce_precision(value, 8, 7)
        return high.astype(BF16), (value - high).astype(BF16)

    n = nocc
    rot_own = pl.pallas_call(
        series_kernel,
        out_shape=jax.ShapeDtypeStruct((n, n // 2), BF16),
        in_specs=[SMEM] + [VMEM] * 4,
        scratch_shapes=[pltpu.VMEM((n, n), BF16)] * 6,
        compiler_params=grant(28),
        name="series",
    )(place, *pair(half), *pair(other))
    rot_other = lax.ppermute(rot_own, "core", swap)
    rotated = pl.pallas_call(
        rotate_kernel,
        out_shape=jax.ShapeDtypeStruct((n, n), BF16),
        in_specs=[SMEM] + [VMEM] * 3,
        compiler_params=grant(16),
        name="rotate",
    )(place, rot_own, rot_other, integrals[0])
    regrouped = lax.all_to_all(rotated.reshape(128, 8, n), BAS, 0, 0, tiled=True)
    new_orbitals = pl.pallas_call(
        orbitals_kernel,
        out_shape=jax.ShapeDtypeStruct((nbas, block), BF16),
        in_specs=[SMEM] + [VMEM] * 3,
        compiler_params=grant(60),
        name="new_orbitals",
    )(place, rot_own, rot_other, met)
    return new_orbitals, regrouped


def solution(mesh):
    split = Mesh(mesh.devices.reshape(8, 8, 2, 4), ("y", "z", "core", "x"))
    return jax.shard_map(
        on_device,
        mesh=split,
        in_specs=(P(BAS, "x"), P(None, BAS, "x"), P(None, "x"), P(BAS, None, "x")),
        out_specs=(P(BAS, "x"), P(None, BAS, "x")),
        check_vma=False,
    )
```

```python
import functools

import jax
import jax.numpy as jnp
from jax import lax
from jax.experimental import pallas as pl
from jax.experimental.pallas import tpu as pltpu
from jax.sharding import Mesh, PartitionSpec as P

F32, BF16, F16 = jnp.float32, jnp.bfloat16, jnp.float16
PLANE = ("y", "z")
BAS = ("y", "z", "core")
WIRE_SCALE = 0.0625
def grant(mib):
    return pltpu.CompilerParams(vmem_limit_bytes=mib << 20)


VMEM = pl.BlockSpec(memory_space=pltpu.VMEM)
SMEM = pl.BlockSpec(memory_space=pltpu.SMEM)


def high_low(value):
    high = value.astype(BF16)
    return high, (value - high.astype(F32)).astype(BF16)


def diagonal_kernel(orb, dip, out):
    for k in range(3):
        part = jnp.sum(orb[...].astype(F32) * dip[k].astype(F32), axis=0, keepdims=True)
        for half in range(2):
            line = jnp.broadcast_to(part[:, 128 * half : 128 * half + 128], (out.shape[0], 128))
            out[:, 2 * k + half] = line
    out[:, 6:8] = jnp.zeros((out.shape[0], 2, 128), F32)


def pack_kernel(parts, orb, out):
    total = jnp.sum(parts[...], axis=0)
    first = total.astype(BF16)
    rest = total - first.astype(F32)
    second = rest.astype(BF16)
    third = (rest - second.astype(F32)).astype(BF16)
    tail = jnp.concatenate([first, second, third, jnp.zeros((8, 128), BF16)], axis=0)
    for d in range(out.shape[0]):
        out[d, 0, :128] = orb[:, :128]
        out[d, 1, :128] = orb[:, 128:]
        out[d, 0, 128:] = tail
        out[d, 1, 128:] = jnp.zeros((32, 128), BF16)


def gradient_kernel(scale, place, met, met_other, d_own, d_other, out):
    core, orb = place[0], place[1]
    contract = (((0,), (0,)), ((), ()))

    def centers(block):
        total = jnp.zeros((8, 128), F32)
        for source in (met, met_other):
            tail = source[block, 0, 128:].astype(F32)
            total = total + (tail[0:8] + tail[8:16] + tail[16:24])
        return total

    mine = centers(orb)
    turned = mine.T
    cen_j = [jnp.concatenate([turned[:, 2 * k : 2 * k + 1], turned[:, 2 * k + 1 : 2 * k + 2]], axis=0) for k in range(3)]
    for half in range(2):
        block = 2 * core + half
        cen_i = centers(block)
        for g in range(2):
            total = None
            for k in range(3):
                moment = lax.dot_general(d_own[k], met[block, g, :128], contract, preferred_element_type=F32)
                moment += lax.dot_general(
                    d_other[k], met_other[block, g, :128], contract, preferred_element_type=F32
                )
                term = moment * (cen_i[2 * k + g : 2 * k + g + 1] - cen_j[k])
                total = term if total is None else total + term
            total = total * scale
            for r in range(16):
                out[4 * r + 2 * half + g] = total[16 * r : 16 * r + 16]


def product(left_h, left_l, right_h, right_l):
    dot = functools.partial(jnp.dot, preferred_element_type=F32)
    return dot(left_h, right_h) + (dot(left_h, right_l) + dot(left_l, right_h))


def series_kernel(place, own_h, own_l, other_h, other_l, rot, xh, xl, x2h, x2l, qh, ql):
    n, tile = 1024, 512
    core = place[0]
    for src_h, src_l, half in ((own_h, own_l, core), (other_h, other_l, 1 - core)):
        for g in range(4):
            cols = pl.ds(pl.multiple_of(half * 512 + 128 * g, 128), 128)
            for xi in range(4):
                for r in range(16):
                    rows = slice(256 * xi + 16 * r, 256 * xi + 16 * r + 16)
                    xh[rows, cols] = src_h[xi, 4 * r + g]
                    xl[rows, cols] = src_l[xi, 4 * r + g]

    def one(first):
        row = lax.broadcasted_iota(jnp.int32, (n, tile), 0)
        col = lax.broadcasted_iota(jnp.int32, (n, tile), 1) + first
        return (row == col).astype(F32)

    def linear(cols):
        return xh[:, cols].astype(F32) + xl[:, cols].astype(F32)

    @pl.loop(0, n // tile)
    def _(step):
        cols = pl.ds(pl.multiple_of(step * tile, tile), tile)
        square = product(xh[...], xl[...], xh[:, cols], xl[:, cols])
        x2h[:, cols], x2l[:, cols] = high_low(square)
        qh[:, cols], ql[:, cols] = high_low(
            one(step * tile) * (1 / 24) + linear(cols) * (1 / 120) + square * (1 / 720)
        )

    @pl.loop(0, 512 // tile)
    def _(step):
        first = core * 512 + step * tile
        cols = pl.ds(pl.multiple_of(first, tile), tile)
        inner = product(x2h[...], x2l[...], qh[:, cols], ql[:, cols])
        qh[:, cols], ql[:, cols] = high_low(one(first) * 0.5 + linear(cols) * (1 / 6) + inner)

    @pl.loop(0, 512 // tile)
    def _(step):
        first = core * 512 + step * tile
        cols = pl.ds(pl.multiple_of(first, tile), tile)
        outer = product(x2h[...], x2l[...], qh[:, cols], ql[:, cols])
        rot[:, pl.ds(pl.multiple_of(step * tile, tile), tile)] = (one(first) + linear(cols) + outer).astype(BF16)


def near_kernel(place, rot_own, integrals, out):
    tile = 512
    near = pl.ds(pl.multiple_of(place[0] * 512, 512), 512)

    @pl.loop(0, 1024 // tile)
    def _(step):
        cols = pl.ds(pl.multiple_of(step * tile, tile), tile)
        out[:, cols] = jnp.dot(rot_own[...], integrals[near, cols], preferred_element_type=F32)


def rotate_kernel(place, near_part, rot_other, integrals, out):
    tile = 512
    far = pl.ds(pl.multiple_of(512 - place[0] * 512, 512), 512)

    @pl.loop(0, 1024 // tile)
    def _(step):
        cols = pl.ds(pl.multiple_of(step * tile, tile), tile)
        total = jnp.dot(rot_other[...], integrals[far, cols], preferred_element_type=F32)
        out[:, cols] = (near_part[:, cols] + total).astype(BF16)


def orbitals_kernel(place, rot_own, rot_other, met, out):
    core, orb = place[0], place[1]
    rows = pl.ds(pl.multiple_of(orb * 256, 256), 256)
    total = None
    for rot, half in ((rot_own, core), (rot_other, 1 - core)):
        mine = rot[rows, :]
        for h in range(2):
            for g in range(2):
                first = 256 * h + 128 * g
                part = lax.dot_general(
                    met[2 * half + h, g, :128], mine[:, first : first + 128],
                    (((1,), (1,)), ((), ())), preferred_element_type=F32,
                )
                total = part if total is None else total + part
    out[...] = total.astype(BF16)


def on_device(orbitals, dipole_orbitals, generator, integrals):
    nbas, block = orbitals.shape
    nocc = generator.shape[0]
    scale = 4.0 / (16.0 * nocc**0.5)
    core, orb_index = lax.axis_index("core"), lax.axis_index("x")
    spot = lax.axis_index("y") * 8 + lax.axis_index("z")
    place = jnp.stack([core, orb_index]).astype(jnp.int32)
    swap = [(0, 1), (1, 0)]

    def spread(value, axes, count):
        copies = jnp.broadcast_to(value[None], (count,) + value.shape)
        return lax.all_to_all(copies, axes, 0, 0, tiled=True)

    partial = pl.pallas_call(
        diagonal_kernel, out_shape=jax.ShapeDtypeStruct((64, 8, 128), F32), name="diagonal"
    )(orbitals, dipole_orbitals)
    partial, d_here, given = lax.optimization_barrier((partial, dipole_orbitals, generator))
    centers = lax.all_to_all(partial, PLANE, 0, 0, tiled=True)
    d_other = lax.ppermute(d_here, "core", swap)
    centers, d_other = lax.optimization_barrier((centers, d_other))
    given = lax.dynamic_slice(given, (core * 512 + (spot % 4) * 128, (spot // 4) * 16), (128, 16)).astype(F32).T
    packed = pl.pallas_call(
        pack_kernel, out_shape=jax.ShapeDtypeStruct((4, 2, nbas + 32, 128), BF16), compiler_params=grant(6), name="pack"
    )(centers, orbitals)
    packed, d_here, given = lax.optimization_barrier((packed, d_here, given))
    met = lax.all_to_all(packed, "x", 0, 0, tiled=True)
    met_other = lax.ppermute(met, "core", swap)
    pieces = pl.pallas_call(
        functools.partial(gradient_kernel, scale),
        out_shape=jax.ShapeDtypeStruct((64, 16, 128), F32),
        in_specs=[SMEM] + [VMEM] * 4,
        compiler_params=grant(8),
        name="gradient",
    )(place, met, met_other, d_here, d_other)
    piece = jnp.sum(lax.all_to_all(pieces, PLANE, 0, 0, tiled=True), axis=0) + given
    wire = (piece * WIRE_SCALE).astype(F16)
    half = spread(spread(wire, PLANE, 64), "x", 4)
    other = lax.ppermute(half, "core", swap)

    def pair(value):
        value = value.astype(F32) * (1 / WIRE_SCALE)
        high = lax.reduce_precision(value, 8, 7)
        return high.astype(BF16), (value - high).astype(BF16)

    n = nocc
    rot_own = pl.pallas_call(
        series_kernel,
        out_shape=jax.ShapeDtypeStruct((n, n // 2), BF16),
        in_specs=[SMEM] + [VMEM] * 4,
        scratch_shapes=[pltpu.VMEM((n, n), BF16)] * 6,
        compiler_params=grant(28),
        name="series",
    )(place, *pair(half), *pair(other))
    rot_other = lax.ppermute(rot_own, "core", swap)
    near_part = pl.pallas_call(
        near_kernel,
        out_shape=jax.ShapeDtypeStruct((n, n), F32),
        in_specs=[SMEM] + [VMEM] * 2,
        compiler_params=grant(16),
        cost_estimate=pl.CostEstimate(flops=1 << 30, bytes_accessed=7 << 20, transcendentals=0),
        name="near",
    )(place, rot_own, integrals[0])
    rotated = pl.pallas_call(
        rotate_kernel,
        out_shape=jax.ShapeDtypeStruct((n, n), BF16),
        in_specs=[SMEM] + [VMEM] * 3,
        compiler_params=grant(16),
        name="rotate",
    )(place, near_part, rot_other, integrals[0])
    regrouped = lax.all_to_all(rotated.reshape(128, 8, n), BAS, 0, 0, tiled=True)
    new_orbitals = pl.pallas_call(
        orbitals_kernel,
        out_shape=jax.ShapeDtypeStruct((nbas, block), BF16),
        in_specs=[SMEM] + [VMEM] * 3,
        compiler_params=grant(60),
        name="new_orbitals",
    )(place, rot_own, rot_other, met)
    return new_orbitals, regrouped


def solution(mesh):
    split = Mesh(mesh.devices.reshape(8, 8, 2, 4), ("y", "z", "core", "x"))
    return jax.shard_map(
        on_device,
        mesh=split,
        in_specs=(P(BAS, "x"), P(None, BAS, "x"), P(None, "x"), P(BAS, None, "x")),
        out_specs=(P(BAS, "x"), P(None, BAS, "x")),
        check_vma=False,
    )
```

```python
import functools

import jax
import jax.numpy as jnp
from jax import lax
from jax.experimental import pallas as pl
from jax.experimental.pallas import tpu as pltpu
from jax.sharding import Mesh, PartitionSpec as P

F32, BF16, F16 = jnp.float32, jnp.bfloat16, jnp.float16
PLANE = ("y", "z")
BAS = ("y", "z", "core")
WIRE_SCALE = 0.0625
def grant(mib):
    return pltpu.CompilerParams(vmem_limit_bytes=mib << 20)


VMEM = pl.BlockSpec(memory_space=pltpu.VMEM)
SMEM = pl.BlockSpec(memory_space=pltpu.SMEM)


def high_low(value):
    high = value.astype(BF16)
    return high, (value - high.astype(F32)).astype(BF16)


def diagonal_kernel(orb, dip, out):
    for k in range(3):
        part = jnp.sum(orb[...].astype(F32) * dip[k].astype(F32), axis=0, keepdims=True)
        for half in range(2):
            line = jnp.broadcast_to(part[:, 128 * half : 128 * half + 128], (out.shape[0], 128))
            out[:, 2 * k + half] = line
    out[:, 6:8] = jnp.zeros((out.shape[0], 2, 128), F32)


def pack_kernel(parts, orb, out):
    total = jnp.sum(parts[...], axis=0)
    first = total.astype(BF16)
    rest = total - first.astype(F32)
    second = rest.astype(BF16)
    third = (rest - second.astype(F32)).astype(BF16)
    tail = jnp.concatenate([first, second, third, jnp.zeros((8, 128), BF16)], axis=0)
    for d in range(out.shape[0]):
        out[d, 0, :128] = orb[:, :128]
        out[d, 1, :128] = orb[:, 128:]
        out[d, 0, 128:] = tail
        out[d, 1, 128:] = jnp.zeros((32, 128), BF16)


def gradient_kernel(scale, place, met, met_other, d_own, d_other, out):
    core, orb = place[0], place[1]
    contract = (((0,), (0,)), ((), ()))

    def centers(block):
        total = jnp.zeros((8, 128), F32)
        for source in (met, met_other):
            tail = source[block, 0, 128:].astype(F32)
            total = total + (tail[0:8] + tail[8:16] + tail[16:24])
        return total

    mine = centers(orb)
    turned = mine.T
    cen_j = [jnp.concatenate([turned[:, 2 * k : 2 * k + 1], turned[:, 2 * k + 1 : 2 * k + 2]], axis=0) for k in range(3)]
    for half in range(2):
        block = 2 * core + half
        cen_i = centers(block)
        for g in range(2):
            total = None
            for k in range(3):
                moment = lax.dot_general(d_own[k], met[block, g, :128], contract, preferred_element_type=F32)
                moment += lax.dot_general(
                    d_other[k], met_other[block, g, :128], contract, preferred_element_type=F32
                )
                term = moment * (cen_i[2 * k + g : 2 * k + g + 1] - cen_j[k])
                total = term if total is None else total + term
            total = total * scale
            for r in range(16):
                out[4 * r + 2 * half + g] = total[16 * r : 16 * r + 16]


def product(left_h, left_l, right_h, right_l):
    dot = functools.partial(jnp.dot, preferred_element_type=F32)
    return dot(left_h, right_h) + (dot(left_h, right_l) + dot(left_l, right_h))


def assemble(half, src_h, src_l, high, low):
    for g in range(4):
        cols = pl.ds(pl.multiple_of(half * 512 + 128 * g, 128), 128)
        for xi in range(4):
            for r in range(16):
                rows = slice(256 * xi + 16 * r, 256 * xi + 16 * r + 16)
                high[rows, cols] = src_h[xi, 4 * r + g]
                low[rows, cols] = src_l[xi, 4 * r + g]


def square_kernel(place, own_h, own_l, out, high, low):
    assemble(0, own_h, own_l, high, low)
    rows = pl.ds(pl.multiple_of(place[0] * 512, 512), 512)
    out[...] = product(high[...], low[...], high[rows, :], low[rows, :])


def series_kernel(place, near_square, own_h, own_l, other_h, other_l, rot, xh, xl, x2h, x2l, qh, ql):
    n, tile = 1024, 512
    core = place[0]
    assemble(core, own_h, own_l, xh, xl)
    assemble(1 - core, other_h, other_l, xh, xl)
    first = core * tile
    near = pl.ds(pl.multiple_of(first, tile), tile)
    far = pl.ds(pl.multiple_of(tile - first, tile), tile)

    def one():
        row = lax.broadcasted_iota(jnp.int32, (n, tile), 0)
        col = lax.broadcasted_iota(jnp.int32, (n, tile), 1) + first
        return (row == col).astype(F32)

    def linear():
        return xh[:, near].astype(F32) + xl[:, near].astype(F32)

    square = near_square[...] + product(xh[:, far], xl[:, far], xh[far, near], xl[far, near])
    x2h[:, near], x2l[:, near] = high_low(square)
    qh[...], ql[...] = high_low(one() * (1 / 24) + linear() * (1 / 120) + square * (1 / 720))
    x2h[:, far], x2l[:, far] = high_low(product(xh[...], xl[...], xh[:, far], xl[:, far]))
    inner = product(x2h[...], x2l[...], qh[...], ql[...])
    qh[...], ql[...] = high_low(one() * 0.5 + linear() * (1 / 6) + inner)
    outer = product(x2h[...], x2l[...], qh[...], ql[...])
    rot[...] = (one() + linear() + outer).astype(BF16)


def near_kernel(place, rot_own, integrals, out):
    tile = 512
    near = pl.ds(pl.multiple_of(place[0] * 512, 512), 512)

    @pl.loop(0, 1024 // tile)
    def _(step):
        cols = pl.ds(pl.multiple_of(step * tile, tile), tile)
        out[:, cols] = jnp.dot(rot_own[...], integrals[near, cols], preferred_element_type=F32)


def rotate_kernel(place, near_part, rot_other, integrals, out):
    tile = 512
    far = pl.ds(pl.multiple_of(512 - place[0] * 512, 512), 512)

    @pl.loop(0, 1024 // tile)
    def _(step):
        cols = pl.ds(pl.multiple_of(step * tile, tile), tile)
        total = jnp.dot(rot_other[...], integrals[far, cols], preferred_element_type=F32)
        out[:, cols] = (near_part[:, cols] + total).astype(BF16)


def orbitals_kernel(place, rot_own, rot_other, met, out):
    core, orb = place[0], place[1]
    rows = pl.ds(pl.multiple_of(orb * 256, 256), 256)
    total = None
    for rot, half in ((rot_own, core), (rot_other, 1 - core)):
        mine = rot[rows, :]
        for h in range(2):
            for g in range(2):
                first = 256 * h + 128 * g
                part = lax.dot_general(
                    met[2 * half + h, g, :128], mine[:, first : first + 128],
                    (((1,), (1,)), ((), ())), preferred_element_type=F32,
                )
                total = part if total is None else total + part
    out[...] = total.astype(BF16)


def on_device(orbitals, dipole_orbitals, generator, integrals):
    nbas, block = orbitals.shape
    nocc = generator.shape[0]
    scale = 4.0 / (16.0 * nocc**0.5)
    core, orb_index = lax.axis_index("core"), lax.axis_index("x")
    spot = lax.axis_index("y") * 8 + lax.axis_index("z")
    place = jnp.stack([core, orb_index]).astype(jnp.int32)
    swap = [(0, 1), (1, 0)]

    def spread(value, axes, count):
        copies = jnp.broadcast_to(value[None], (count,) + value.shape)
        return lax.all_to_all(copies, axes, 0, 0, tiled=True)

    partial = pl.pallas_call(
        diagonal_kernel, out_shape=jax.ShapeDtypeStruct((64, 8, 128), F32), name="diagonal"
    )(orbitals, dipole_orbitals)
    partial, d_here, given = lax.optimization_barrier((partial, dipole_orbitals, generator))
    centers = lax.all_to_all(partial, PLANE, 0, 0, tiled=True)
    d_other = lax.ppermute(d_here, "core", swap)
    centers, d_other = lax.optimization_barrier((centers, d_other))
    given = lax.dynamic_slice(given, (core * 512 + (spot % 4) * 128, (spot // 4) * 16), (128, 16)).astype(F32).T
    packed = pl.pallas_call(
        pack_kernel, out_shape=jax.ShapeDtypeStruct((4, 2, nbas + 32, 128), BF16), compiler_params=grant(6), name="pack"
    )(centers, orbitals)
    packed, d_here, given = lax.optimization_barrier((packed, d_here, given))
    met = lax.all_to_all(packed, "x", 0, 0, tiled=True)
    met_other = lax.ppermute(met, "core", swap)
    pieces = pl.pallas_call(
        functools.partial(gradient_kernel, scale),
        out_shape=jax.ShapeDtypeStruct((64, 16, 128), F32),
        in_specs=[SMEM] + [VMEM] * 4,
        compiler_params=grant(8),
        name="gradient",
    )(place, met, met_other, d_here, d_other)
    piece = jnp.sum(lax.all_to_all(pieces, PLANE, 0, 0, tiled=True), axis=0) + given
    wire = (piece * WIRE_SCALE).astype(F16)
    half = spread(spread(wire, PLANE, 64), "x", 4)
    other = lax.ppermute(half, "core", swap)

    def pair(value):
        value = value.astype(F32) * (1 / WIRE_SCALE)
        high = lax.reduce_precision(value, 8, 7)
        return high.astype(BF16), (value - high).astype(BF16)

    n = nocc
    own_pair = pair(half)
    near_square = pl.pallas_call(
        square_kernel,
        out_shape=jax.ShapeDtypeStruct((n, n // 2), F32),
        in_specs=[SMEM] + [VMEM] * 2,
        scratch_shapes=[pltpu.VMEM((n, n // 2), BF16)] * 2,
        compiler_params=grant(12),
        cost_estimate=pl.CostEstimate(flops=3 << 29, bytes_accessed=4 << 20, transcendentals=0),
        name="square",
    )(place, *own_pair)
    rot_own = pl.pallas_call(
        series_kernel,
        out_shape=jax.ShapeDtypeStruct((n, n // 2), BF16),
        in_specs=[SMEM] + [VMEM] * 5,
        scratch_shapes=[pltpu.VMEM((n, n), BF16)] * 4 + [pltpu.VMEM((n, n // 2), BF16)] * 2,
        compiler_params=grant(28),
        name="series",
    )(place, near_square, *own_pair, *pair(other))
    rot_other = lax.ppermute(rot_own, "core", swap)
    near_part = pl.pallas_call(
        near_kernel,
        out_shape=jax.ShapeDtypeStruct((n, n), F32),
        in_specs=[SMEM] + [VMEM] * 2,
        compiler_params=grant(16),
        cost_estimate=pl.CostEstimate(flops=1 << 30, bytes_accessed=7 << 20, transcendentals=0),
        name="near",
    )(place, rot_own, integrals[0])
    rotated = pl.pallas_call(
        rotate_kernel,
        out_shape=jax.ShapeDtypeStruct((n, n), BF16),
        in_specs=[SMEM] + [VMEM] * 3,
        compiler_params=grant(16),
        name="rotate",
    )(place, near_part, rot_other, integrals[0])
    regrouped = lax.all_to_all(rotated.reshape(128, 8, n), BAS, 0, 0, tiled=True)
    new_orbitals = pl.pallas_call(
        orbitals_kernel,
        out_shape=jax.ShapeDtypeStruct((nbas, block), BF16),
        in_specs=[SMEM] + [VMEM] * 3,
        compiler_params=grant(60),
        name="new_orbitals",
    )(place, rot_own, rot_other, met)
    return new_orbitals, regrouped


def solution(mesh):
    split = Mesh(mesh.devices.reshape(8, 8, 2, 4), ("y", "z", "core", "x"))
    return jax.shard_map(
        on_device,
        mesh=split,
        in_specs=(P(BAS, "x"), P(None, BAS, "x"), P(None, "x"), P(BAS, None, "x")),
        out_specs=(P(BAS, "x"), P(None, BAS, "x")),
        check_vma=False,
    )
```

```python
import functools

import jax
import jax.numpy as jnp
from jax import lax
from jax.experimental import pallas as pl
from jax.experimental.pallas import tpu as pltpu
from jax.sharding import Mesh, PartitionSpec as P

F32, BF16, F16 = jnp.float32, jnp.bfloat16, jnp.float16
PLANE = ("y", "z")
BAS = ("y", "z", "core")
WIRE_SCALE = 0.0625
def grant(mib):
    return pltpu.CompilerParams(vmem_limit_bytes=mib << 20)


VMEM = pl.BlockSpec(memory_space=pltpu.VMEM)
SMEM = pl.BlockSpec(memory_space=pltpu.SMEM)


def high_low(value):
    high = value.astype(BF16)
    return high, (value - high.astype(F32)).astype(BF16)


def diagonal_kernel(orb, dip, out):
    for k in range(3):
        part = jnp.sum(orb[...].astype(F32) * dip[k].astype(F32), axis=0, keepdims=True)
        for half in range(2):
            line = jnp.broadcast_to(part[:, 128 * half : 128 * half + 128], (out.shape[0], 128))
            out[:, 2 * k + half] = line
    out[:, 6:8] = jnp.zeros((out.shape[0], 2, 128), F32)


def pack_kernel(parts, orb, out):
    total = jnp.sum(parts[...], axis=0)
    first = total.astype(BF16)
    rest = total - first.astype(F32)
    second = rest.astype(BF16)
    third = (rest - second.astype(F32)).astype(BF16)
    tails = (
        jnp.concatenate([first, second], axis=0),
        jnp.concatenate([third, jnp.zeros((8, 128), BF16)], axis=0),
    )
    for d in range(out.shape[0]):
        out[d, 0, :128] = orb[:, :128]
        out[d, 1, :128] = orb[:, 128:]
        out[d, 0, 128:] = tails[0]
        out[d, 1, 128:] = tails[1]


CONTRACT = (((0,), (0,)), ((), ()))


def moment_kernel(place, met, d_own, out):
    for half in range(2):
        for g in range(2):
            for k in range(3):
                rows = met[2 * place[0] + half, g, :128]
                out[k, 2 * half + g] = lax.dot_general(d_own[k], rows, CONTRACT, preferred_element_type=F32)


def gradient_kernel(scale, place, met, met_other, near, d_other, out):
    core, orb = place[0], place[1]

    def centers(block):
        total = jnp.zeros((8, 128), F32)
        for source in (met, met_other):
            large, small = source[block, 0, 128:].astype(F32), source[block, 1, 128:].astype(F32)
            total = total + (large[0:8] + large[8:16] + small[0:8])
        return total

    mine = centers(orb)
    turned = mine.T
    cen_j = [jnp.concatenate([turned[:, 2 * k : 2 * k + 1], turned[:, 2 * k + 1 : 2 * k + 2]], axis=0) for k in range(3)]
    for half in range(2):
        block = 2 * core + half
        cen_i = centers(block)
        for g in range(2):
            total = None
            for k in range(3):
                moment = near[k, 2 * half + g] + lax.dot_general(
                    d_other[k], met_other[block, g, :128], CONTRACT, preferred_element_type=F32
                )
                term = moment * (cen_i[2 * k + g : 2 * k + g + 1] - cen_j[k])
                total = term if total is None else total + term
            total = total * scale
            for r in range(16):
                out[4 * r + 2 * half + g] = total[16 * r : 16 * r + 16]


def product(left_h, left_l, right_h, right_l):
    dot = functools.partial(jnp.dot, preferred_element_type=F32)
    return dot(left_h, right_h) + (dot(left_h, right_l) + dot(left_l, right_h))


def assemble(half, src_h, src_l, high, low):
    for g in range(4):
        cols = pl.ds(pl.multiple_of(half * 512 + 128 * g, 128), 128)
        for xi in range(4):
            for r in range(16):
                rows = slice(256 * xi + 16 * r, 256 * xi + 16 * r + 16)
                high[rows, cols] = src_h[xi, 4 * r + g]
                low[rows, cols] = src_l[xi, 4 * r + g]


def square_kernel(place, own_h, own_l, out, high, low):
    assemble(0, own_h, own_l, high, low)
    rows = pl.ds(pl.multiple_of(place[0] * 512, 512), 512)
    out[...] = product(high[...], low[...], high[rows, :], low[rows, :])


def series_kernel(place, near_square, own_h, own_l, other_h, other_l, rot, xh, xl, x2h, x2l, qh, ql):
    n, tile = 1024, 512
    core = place[0]
    assemble(core, own_h, own_l, xh, xl)
    assemble(1 - core, other_h, other_l, xh, xl)
    first = core * tile
    near = pl.ds(pl.multiple_of(first, tile), tile)
    far = pl.ds(pl.multiple_of(tile - first, tile), tile)

    def one():
        row = lax.broadcasted_iota(jnp.int32, (n, tile), 0)
        col = lax.broadcasted_iota(jnp.int32, (n, tile), 1) + first
        return (row == col).astype(F32)

    def linear():
        return xh[:, near].astype(F32) + xl[:, near].astype(F32)

    square = near_square[...] + product(xh[:, far], xl[:, far], xh[far, near], xl[far, near])
    x2h[:, near], x2l[:, near] = high_low(square)
    qh[...], ql[...] = high_low(one() * (1 / 24) + linear() * (1 / 120) + square * (1 / 720))
    x2h[:, far], x2l[:, far] = high_low(product(xh[...], xl[...], xh[:, far], xl[:, far]))
    inner = product(x2h[...], x2l[...], qh[...], ql[...])
    qh[...], ql[...] = high_low(one() * 0.5 + linear() * (1 / 6) + inner)
    outer = product(x2h[...], x2l[...], qh[...], ql[...])
    rot[...] = (one() + linear() + outer).astype(BF16)


def near_kernel(place, rot_own, integrals, out):
    tile = 512
    near = pl.ds(pl.multiple_of(place[0] * 512, 512), 512)

    @pl.loop(0, 1024 // tile)
    def _(step):
        cols = pl.ds(pl.multiple_of(step * tile, tile), tile)
        out[:, cols] = jnp.dot(rot_own[...], integrals[near, cols], preferred_element_type=F32)


def rotate_kernel(place, near_part, rot_other, integrals, out):
    tile = 512
    far = pl.ds(pl.multiple_of(512 - place[0] * 512, 512), 512)

    @pl.loop(0, 1024 // tile)
    def _(step):
        cols = pl.ds(pl.multiple_of(step * tile, tile), tile)
        total = jnp.dot(rot_other[...], integrals[far, cols], preferred_element_type=F32)
        out[:, cols] = (near_part[:, cols] + total).astype(BF16)


def orbitals_kernel(place, rot_own, rot_other, met, out):
    core, orb = place[0], place[1]
    rows = pl.ds(pl.multiple_of(orb * 256, 256), 256)
    total = None
    for rot, half in ((rot_own, core), (rot_other, 1 - core)):
        mine = rot[rows, :]
        for h in range(2):
            for g in range(2):
                first = 256 * h + 128 * g
                part = lax.dot_general(
                    met[2 * half + h, g, :128], mine[:, first : first + 128],
                    (((1,), (1,)), ((), ())), preferred_element_type=F32,
                )
                total = part if total is None else total + part
    out[...] = total.astype(BF16)


def on_device(orbitals, dipole_orbitals, generator, integrals):
    nbas, block = orbitals.shape
    nocc = generator.shape[0]
    scale = 4.0 / (16.0 * nocc**0.5)
    core, orb_index = lax.axis_index("core"), lax.axis_index("x")
    spot = lax.axis_index("y") * 8 + lax.axis_index("z")
    place = jnp.stack([core, orb_index]).astype(jnp.int32)
    swap = [(0, 1), (1, 0)]

    def spread(value, axes, count):
        copies = jnp.broadcast_to(value[None], (count,) + value.shape)
        return lax.all_to_all(copies, axes, 0, 0, tiled=True)

    partial = pl.pallas_call(
        diagonal_kernel, out_shape=jax.ShapeDtypeStruct((64, 8, 128), F32), name="diagonal"
    )(orbitals, dipole_orbitals)
    partial, d_here, given = lax.optimization_barrier((partial, dipole_orbitals, generator))
    centers = lax.all_to_all(partial, PLANE, 0, 0, tiled=True)
    d_other = lax.ppermute(d_here, "core", swap)
    centers, d_other = lax.optimization_barrier((centers, d_other))
    given = lax.dynamic_slice(given, (core * 512 + (spot % 4) * 128, (spot // 4) * 16), (128, 16)).astype(F32).T
    packed = pl.pallas_call(
        pack_kernel, out_shape=jax.ShapeDtypeStruct((4, 2, nbas + 16, 128), BF16), compiler_params=grant(6), name="pack"
    )(centers, orbitals)
    packed, d_here, given = lax.optimization_barrier((packed, d_here, given))
    met = lax.all_to_all(packed, "x", 0, 0, tiled=True)
    met_other = lax.ppermute(met, "core", swap)
    near = pl.pallas_call(
        moment_kernel,
        out_shape=jax.ShapeDtypeStruct((3, 4, block, 128), F32),
        in_specs=[SMEM] + [VMEM] * 2,
        compiler_params=grant(8),
        cost_estimate=pl.CostEstimate(flops=1 << 28, bytes_accessed=2 << 20, transcendentals=0),
        name="moments",
    )(place, met, d_here)
    pieces = pl.pallas_call(
        functools.partial(gradient_kernel, scale),
        out_shape=jax.ShapeDtypeStruct((64, 16, 128), F32),
        in_specs=[SMEM] + [VMEM] * 4,
        compiler_params=grant(8),
        name="gradient",
    )(place, met, met_other, near, d_other)
    piece = jnp.sum(lax.all_to_all(pieces, PLANE, 0, 0, tiled=True), axis=0) + given
    wire = (piece * WIRE_SCALE).astype(F16)
    half = spread(spread(wire, PLANE, 64), "x", 4)
    other = lax.ppermute(half, "core", swap)

    def pair(value):
        value = value.astype(F32) * (1 / WIRE_SCALE)
        high = lax.reduce_precision(value, 8, 7)
        return high.astype(BF16), (value - high).astype(BF16)

    n = nocc
    own_pair = pair(half)
    near_square = pl.pallas_call(
        square_kernel,
        out_shape=jax.ShapeDtypeStruct((n, n // 2), F32),
        in_specs=[SMEM] + [VMEM] * 2,
        scratch_shapes=[pltpu.VMEM((n, n // 2), BF16)] * 2,
        compiler_params=grant(12),
        cost_estimate=pl.CostEstimate(flops=3 << 29, bytes_accessed=4 << 20, transcendentals=0),
        name="square",
    )(place, *own_pair)
    rot_own = pl.pallas_call(
        series_kernel,
        out_shape=jax.ShapeDtypeStruct((n, n // 2), BF16),
        in_specs=[SMEM] + [VMEM] * 5,
        scratch_shapes=[pltpu.VMEM((n, n), BF16)] * 4 + [pltpu.VMEM((n, n // 2), BF16)] * 2,
        compiler_params=grant(28),
        name="series",
    )(place, near_square, *own_pair, *pair(other))
    rot_other = lax.ppermute(rot_own, "core", swap)
    near_part = pl.pallas_call(
        near_kernel,
        out_shape=jax.ShapeDtypeStruct((n, n), F32),
        in_specs=[SMEM] + [VMEM] * 2,
        compiler_params=grant(16),
        cost_estimate=pl.CostEstimate(flops=1 << 30, bytes_accessed=7 << 20, transcendentals=0),
        name="near",
    )(place, rot_own, integrals[0])
    rotated = pl.pallas_call(
        rotate_kernel,
        out_shape=jax.ShapeDtypeStruct((n, n), BF16),
        in_specs=[SMEM] + [VMEM] * 3,
        compiler_params=grant(16),
        name="rotate",
    )(place, near_part, rot_other, integrals[0])
    regrouped = lax.all_to_all(rotated.reshape(128, 8, n), BAS, 0, 0, tiled=True)
    new_orbitals = pl.pallas_call(
        orbitals_kernel,
        out_shape=jax.ShapeDtypeStruct((nbas, block), BF16),
        in_specs=[SMEM] + [VMEM] * 3,
        compiler_params=grant(60),
        name="new_orbitals",
    )(place, rot_own, rot_other, met)
    return new_orbitals, regrouped


def solution(mesh):
    split = Mesh(mesh.devices.reshape(8, 8, 2, 4), ("y", "z", "core", "x"))
    return jax.shard_map(
        on_device,
        mesh=split,
        in_specs=(P(BAS, "x"), P(None, BAS, "x"), P(None, "x"), P(BAS, None, "x")),
        out_specs=(P(BAS, "x"), P(None, BAS, "x")),
        check_vma=False,
    )
```
